32 devices in a mesh: groups: 1, lat: 16 (over z, y, x), ckpt: 2 (over core).
Axes of the slice: x: 2, y: 2, z: 4, core: 2. Of those that a mesh axis runs over, the one named last changes fastest.
Arguments:
- inputs: bfloat16 [2, 512, 4096], P('ckpt', ('groups', 'lat')), may hold values from -6 to 6
- enc_weight: bfloat16 [2, 4096, 32768], P('ckpt', None, 'lat'), may hold values from -0.0625 to 0.0625
- enc_bias: float32 [32768], P('lat'), may hold values from -3 to 3
- dec_weight: bfloat16 [2, 4096, 32768], P('ckpt', 'lat'), may hold values from -0.375 to 0.375
- dec_bias: float32 [2, 4096], P('ckpt', 'lat'), may hold values from -3 to 3
- block_ids: int32 [4, 16], P('groups'), may hold values from 0 to 31
- live: int32 [4, 16], P('groups'), may hold values 0 or 1
Outputs:
- recon: bfloat16 [2, 4096, 512], P('ckpt', 'lat', 'groups')
The draws below stay inside these ranges and needn't reach their ends.
Inputs may be any that keep to these rules, and one draw needn't show every extreme that they name: block_ids numbers a block among the 32 blocks of its owner; it matters only where live is 1. live is the count of active blocks of an owner in a tile.
All inputs are finite; a program needn't handle non-finite values.
Results may differ from the reference program's by a relative error of at most 0.0047.
Values may be sent and summed in bfloat16 or wider, within the bound.
No kernel may reach another device: no remote copies, remote signals or barrier semaphores. Data moves between devices by JAX's collectives and lax.ppermute only.
A program may use at most 128 MiB of HBM per device.

```python
import jax
import jax.numpy as jnp

D = 4096
LATENTS = 32768
BLOCK = 64
CKPTS = 2
TILE = 128
TILES = 4
TOKENS = 512
BLK_OWN = 32
N_LAT = 16


def touch_ends(values, own_key, smallest, high):
    extent = values.shape
    index_at = [jax.random.randint(jax.random.fold_in(own_key, axis), (), 0, extent[axis]) for axis in range(len(extent))]
    values = values.at[tuple(index_at)].set(smallest)
    longest = extent.index(max(extent))
    index_at[longest] = (index_at[longest] + 1) % extent[longest]
    return values.at[tuple(index_at)].set(high)


def level_of(own_key, dims, split, least, largest):
    def one(position, blocks):
        draws = jax.random.uniform(jax.random.fold_in(jax.random.fold_in(own_key, 6), position), (blocks,), jnp.float32, least / len(split), largest / len(split))
        return jnp.repeat(jnp.exp(draws), dims[position] // blocks).reshape((-1,) + (1,) * (len(dims) - position - 1))

    factor_of = one(*split[0])
    for cut in split[1:]:
        factor_of = factor_of * one(*cut)
    return factor_of


def centred(key, dims, scale, most, split=(), kind=jnp.bfloat16):
    factor_of = level_of(key, dims, split, -0.22, 0.18) if split else 1.0
    entries = jax.random.normal(key, dims, jnp.float32) * scale * factor_of
    return jnp.minimum(jnp.maximum(entries, -most), most).astype(kind)


def setup_inputs(seed: int = 0, part: int = 0) -> dict:
    streams_of = jax.random.split(jax.random.key(seed), 8)
    part_keys = jax.random.split(jax.random.fold_in(streams_of[7], part), 8)
    inputs = centred(part_keys[0], (CKPTS, TOKENS, D), 1.0, 6.0, ((0, 2), (1, 16)))
    enc_weight = centred(streams_of[1], (CKPTS, D, LATENTS), (CKPTS * D) ** -0.5, 0.0625, ((0, 2), (2, 16)))
    enc_bias = centred(streams_of[2], (LATENTS,), 0.5, 3.0, ((0, 16),), jnp.float32)
    dec_weight = centred(streams_of[3], (CKPTS, D, LATENTS), (N_LAT * BLOCK // 4) ** -0.5, 0.375, ((0, 2), (1, 16)))
    dec_bias = centred(streams_of[4], (CKPTS, D), 0.5, 3.0, ((0, 2), (1, 16)), jnp.float32)
    block_ids = touch_ends(jax.random.randint(part_keys[5], (TILES, N_LAT), 0, BLK_OWN), jax.random.fold_in(part_keys[5], 1), 0, BLK_OWN - 1).astype(jnp.int32)
    live = touch_ends((jax.random.randint(part_keys[6], (TILES, N_LAT), 0, 2) < 1).astype(jnp.int32), jax.random.fold_in(part_keys[6], 1), 0, 1)
    return dict(inputs=inputs, enc_weight=enc_weight, enc_bias=enc_bias, dec_weight=dec_weight, dec_bias=dec_bias, block_ids=block_ids, live=live)


def reference(inputs, enc_weight, enc_bias, dec_weight, dec_bias, block_ids, live):
    preact = jnp.dot(inputs[0], enc_weight[0], preferred_element_type=jnp.float32)
    for index in range(1, CKPTS):
        preact = preact + jnp.dot(inputs[index], enc_weight[index], preferred_element_type=jnp.float32)
    preact = preact + enc_bias[None, :]
    latent = jnp.arange(LATENTS, dtype=jnp.int32)
    owner = latent // (BLK_OWN * BLOCK)
    within = (latent // BLOCK) % BLK_OWN
    active = (live[:, owner] == 1) & (block_ids[:, owner] == within[None, :])
    active = jnp.repeat(active, TILE, axis=0)
    acts = jnp.where(active, jnp.maximum(preact, 0.0), 0.0).astype(jnp.bfloat16)
    acts_cols = jnp.transpose(acts)
    outputs = []
    for index in range(CKPTS):
        single = jnp.dot(dec_weight[index], acts_cols, preferred_element_type=jnp.float32) + dec_bias[index][:, None]
        outputs.append(single.astype(jnp.bfloat16))
    return jnp.stack(outputs)
```

```python
import functools

import jax
import jax.numpy as jnp
from jax import lax
from jax.experimental import pallas as pl
from jax.experimental.pallas import tpu as pltpu
from jax.sharding import PartitionSpec as P

BLOCK = 64
TILE = 128
PAIR = 2 * BLOCK
F32 = jnp.float32
BF16 = jnp.bfloat16
VMEM_BYTES = 24 * 1024 * 1024
VMEM_WEIGHTS = 52 * 1024 * 1024


def body_any(inputs, enc_weight, enc_bias, dec_weight, dec_bias, block_ids, live):
    lat_count = lax.axis_size("lat")
    lat_index = lax.axis_index("lat")
    lat_dev = enc_weight.shape[2]
    own_blocks = lat_dev // BLOCK
    local_ckpts = dec_weight.shape[0]
    features = dec_weight.shape[1]
    preact = jnp.einsum(
        "cdl,crd->lr",
        enc_weight,
        lax.all_gather(inputs, "lat", axis=1, tiled=True),
        preferred_element_type=F32,
    )
    token_count = preact.shape[1]
    tiles = token_count // TILE
    own_ids = lax.dynamic_slice_in_dim(block_ids, lat_index, 1, 1)[:, 0]
    own_live = lax.dynamic_slice_in_dim(live, lat_index, 1, 1)[:, 0]
    choose = (own_ids[:, None] == jnp.arange(own_blocks, dtype=jnp.int32)[None, :]) & (own_live[:, None] == 1)
    choose_cols = jnp.transpose(choose.astype(F32))
    grouped_vals = preact.reshape(own_blocks, BLOCK, tiles, TILE)
    picked = jnp.sum(grouped_vals * choose_cols[:, None, :, None], axis=0)
    picked_bias = jnp.einsum("pe,pt->et", enc_bias.reshape(own_blocks, BLOCK), choose_cols, precision=lax.Precision.HIGHEST)
    summed = lax.psum(picked, "ckpt") + picked_bias[:, :, None]
    acts = jnp.transpose(jnp.maximum(summed, 0.0), (1, 0, 2)).astype(BF16)
    onehot = (
        (block_ids[:, :, None] == jnp.arange(own_blocks, dtype=jnp.int32)[None, None, :]) & (live[:, :, None] == 1)
    ).astype(BF16)
    grouped = dec_weight.reshape(local_ckpts, features, lat_count, own_blocks, BLOCK)
    selected = jnp.einsum("tnp,cdnpe->cdtne", onehot, grouped, preferred_element_type=F32).astype(BF16)
    total = jnp.einsum(
        "ntes,cdtne->cdts",
        lax.all_gather(acts[None], "lat", axis=0, tiled=True),
        selected,
        preferred_element_type=F32,
    )
    recon = total.reshape(local_ckpts, features, token_count)
    return (recon + dec_bias[:, :, None]).astype(BF16)


def block_at(ids_ref, tile, owner, owners):
    return ids_ref[tile * owners + owner]


def swap_halves(values):
    return pltpu.roll(values.astype(F32), BLOCK, 1).astype(BF16)


def send_columns_kernel(ids_ref, at_ref, first_ref, second_ref, out_ref, *, owners):
    lat = at_ref[0]
    plane = lat // 4
    lane = lax.broadcasted_iota(jnp.int32, (first_ref.shape[0], PAIR), 1)
    odd_first = block_at(ids_ref, plane ^ 1, lat, owners) % 2
    odd_second = block_at(ids_ref, plane ^ 3, lat, owners) % 2
    first = first_ref[...].astype(F32)
    second = second_ref[...].astype(F32)
    first = jnp.where(odd_first == 1, pltpu.roll(first, BLOCK, 1), first)
    second = jnp.where(odd_second == 0, pltpu.roll(second, BLOCK, 1), second)
    out_ref[...] = jnp.where(lane < BLOCK, first, second).astype(BF16)


def send_columns(ids, at, enc_weight, owners):
    depth = enc_weight.shape[0]
    step = 1024

    def pick(mask):
        def index(i, ids_ref, at_ref):
            lat = at_ref[0]
            return i, block_at(ids_ref, (lat // 4) ^ mask, lat, owners) // 2

        return index

    return pl.pallas_call(
        functools.partial(send_columns_kernel, owners=owners),
        out_shape=jax.ShapeDtypeStruct((depth, PAIR), BF16),
        grid_spec=pltpu.PrefetchScalarGridSpec(
            num_scalar_prefetch=2,
            grid=(depth // step,),
            in_specs=[pl.BlockSpec((step, PAIR), pick(1)), pl.BlockSpec((step, PAIR), pick(3))],
            out_specs=pl.BlockSpec((step, PAIR), lambda i, ids_ref, at_ref: (i, 0)),
        ),
        compiler_params=pltpu.CompilerParams(vmem_limit_bytes=VMEM_WEIGHTS),
        cost_estimate=pl.CostEstimate(flops=0, bytes_accessed=3 * depth * PAIR * 2, transcendentals=0),
        name="send_columns",
    )(ids, at, enc_weight, enc_weight)


def encode_kernel(ids_ref, live_ref, at_ref, *refs, owners):
    near = refs[0:4]
    far = refs[4:8]
    near_w, far_w, partner_w, bias_ref, out_ref, acc_ref, turn_ref = refs[8:]
    step = pl.program_id(0)

    @pl.when(step == 0)
    def _():
        acc_ref[...] = jnp.zeros_like(acc_ref)

    for index, (tokens, own_w) in enumerate(((near, near_w), (far, far_w))):
        rows = jnp.concatenate([ref[...] for ref in tokens], axis=0)
        columns = jnp.concatenate([own_w[...], partner_w[...]], axis=1)
        acc_ref[index] += jnp.dot(rows, columns, preferred_element_type=F32)

    @pl.when(step == pl.num_programs(0) - 1)
    def _():
        lat = at_ref[0]
        plane, place = lat // 4, lat % 4
        shard = TILE // 4
        for index in range(2):
            tile = plane ^ (2 * index)
            for turn in range(4):
                turn_ref[pl.ds(pl.multiple_of((place ^ turn) * shard, shard), shard), :] = acc_ref[
                    index, turn * shard : (turn + 1) * shard, :
                ]
            acc_ref[index, :PAIR, :PAIR] = jnp.transpose(turn_ref[:, :PAIR])
            acc_ref[index, :PAIR, PAIR:] = jnp.transpose(turn_ref[:, PAIR:])
            odd = block_at(ids_ref, tile, lat, owners) % 2
            own = acc_ref[index, pl.ds(pl.multiple_of(odd * BLOCK, BLOCK), BLOCK), :PAIR]
            other = acc_ref[index, index * BLOCK : (index + 1) * BLOCK, PAIR:]
            own_live = live_ref[tile * owners + lat] == 1
            other_live = live_ref[tile * owners + (lat ^ 4)] == 1
            out_ref[index] = jnp.where(own_live, own + bias_ref[index], 0.0)
            out_ref[2 + index] = jnp.where(other_live, other + bias_ref[2 + index], 0.0)


def encode(ids, live, at, near, far, enc_weight, partner, bias, owners):
    depth = enc_weight.shape[0]
    step = 1024
    shard = near[0].shape[0]

    def pick(mask):
        def index(i, ids_ref, live_ref, at_ref):
            lat = at_ref[0]
            return i, block_at(ids_ref, (lat // 4) ^ mask, lat, owners) // 2

        return index

    tokens = pl.BlockSpec((shard, step), lambda i, *_: (0, i))
    whole = pl.BlockSpec((4, BLOCK, TILE), lambda i, *_: (0, 0, 0))
    return pl.pallas_call(
        functools.partial(encode_kernel, owners=owners),
        out_shape=jax.ShapeDtypeStruct((4, BLOCK, TILE), F32),
        grid_spec=pltpu.PrefetchScalarGridSpec(
            num_scalar_prefetch=3,
            grid=(depth // step,),
            in_specs=[tokens] * 8
            + [
                pl.BlockSpec((step, PAIR), pick(0)),
                pl.BlockSpec((step, PAIR), pick(2)),
                pl.BlockSpec((step, PAIR), lambda i, *_: (i, 0)),
                whole,
            ],
            out_specs=whole,
            scratch_shapes=[pltpu.VMEM((2, TILE, 2 * PAIR), F32), pltpu.VMEM((TILE, 2 * PAIR), F32)],
        ),
        compiler_params=pltpu.CompilerParams(vmem_limit_bytes=VMEM_WEIGHTS),
        cost_estimate=pl.CostEstimate(flops=4 * TILE * depth * 2 * PAIR, bytes_accessed=5 * 2**20, transcendentals=0),
        name="encode",
    )(ids, live, at, *near, *far, enc_weight, enc_weight, partner, bias)


def stage_decoder_kernel(ids_ref, *refs):
    for owner, ref in enumerate(refs[:-1]):
        refs[-1][0, :, owner * PAIR : (owner + 1) * PAIR] = ref[...]


def stage_decoder(ids, dec_weight, owners, tiles):
    features = dec_weight.shape[0]
    per_owner = dec_weight.shape[1] // owners // PAIR

    def pick(owner):
        return lambda t, ids_ref: (0, owner * per_owner + block_at(ids_ref, t, owner, owners) // 2)

    return pl.pallas_call(
        stage_decoder_kernel,
        out_shape=jax.ShapeDtypeStruct((tiles, features, owners * PAIR), BF16),
        grid_spec=pltpu.PrefetchScalarGridSpec(
            num_scalar_prefetch=1,
            grid=(tiles,),
            in_specs=[pl.BlockSpec((features, PAIR), pick(owner)) for owner in range(owners)],
            out_specs=pl.BlockSpec((1, features, owners * PAIR), lambda t, ids_ref: (t, 0, 0)),
        ),
        compiler_params=pltpu.CompilerParams(vmem_limit_bytes=VMEM_WEIGHTS),
        cost_estimate=pl.CostEstimate(
            flops=0, bytes_accessed=2 * tiles * features * owners * PAIR * 2, transcendentals=0
        ),
        name="stage_decoder",
    )(ids, *([dec_weight] * owners))


def decode_kernel(ids_ref, at_ref, *refs, owners):
    mine = refs[0:4]
    theirs = refs[4:8]
    columns_ref, bias_ref, out_ref, acts_ref = refs[8:]
    tile_now = pl.program_id(0)

    @pl.when(tile_now == 0)
    def _():
        lat, core = at_ref[0], at_ref[1]
        for place in range(4):
            for ref, holder in ((mine[place], core), (theirs[place], 1 - core)):
                slots = ((0, holder), (4 + 8 * holder, 0), (4 + 8 * holder, 1), (8, holder))
                for slot, (mask, which) in enumerate(slots):
                    source = lat ^ place ^ mask
                    owner = source ^ (4 * which)
                    for index in range(2):
                        tile = (source // 4) ^ (2 * index)
                        odd = block_at(ids_ref, tile, owner, owners) % 2
                        values = ref[slot, index]
                        zeros = jnp.zeros_like(values)
                        row = pl.multiple_of((tile * owners + owner) * PAIR, PAIR)
                        acts_ref[pl.ds(row, PAIR), :] = jnp.concatenate(
                            [jnp.where(odd == 0, values, zeros), jnp.where(odd == 1, values, zeros)], axis=0
                        )

    rows = owners * PAIR
    acts = acts_ref[pl.ds(pl.multiple_of(tile_now * rows, rows), rows), :]
    total = jnp.dot(columns_ref[0], acts, preferred_element_type=F32)
    out_ref[...] = (total + bias_ref[...]).astype(BF16)


def decode(ids, at, mine, theirs, columns, dec_bias, owners):
    tiles, features, depth = columns.shape
    payload = pl.BlockSpec(mine[0].shape, lambda t, *_: (0, 0, 0, 0))
    return pl.pallas_call(
        functools.partial(decode_kernel, owners=owners),
        out_shape=jax.ShapeDtypeStruct((features, tiles * TILE), BF16),
        grid_spec=pltpu.PrefetchScalarGridSpec(
            num_scalar_prefetch=2,
            grid=(tiles,),
            in_specs=[payload] * 8
            + [
                pl.BlockSpec((1, features, depth), lambda t, *_: (t, 0, 0)),
                pl.BlockSpec((features, 1), lambda t, *_: (0, 0)),
            ],
            out_specs=pl.BlockSpec((features, TILE), lambda t, *_: (0, t)),
            scratch_shapes=[pltpu.VMEM((tiles * depth, TILE), BF16)],
        ),
        compiler_params=pltpu.CompilerParams(vmem_limit_bytes=VMEM_BYTES),
        cost_estimate=pl.CostEstimate(
            flops=2 * tiles * features * depth * TILE, bytes_accessed=6 * 2**20, transcendentals=0
        ),
        name="decode",
    )(ids, at, *mine, *theirs, columns, dec_bias)


def body_planes(inputs, enc_weight, enc_bias, dec_weight, dec_bias, block_ids, live):
    owners = lax.axis_size("lat")
    lat = lax.axis_index("lat")
    core = lax.axis_index("ckpt")
    tiles = block_ids.shape[0]
    own_blocks = enc_weight.shape[2] // BLOCK
    at = jnp.stack([lat, core]).astype(jnp.int32)
    ids = block_ids.reshape(-1)
    alive = live.reshape(-1)

    def swap(values, mask):
        return lax.ppermute(values, "lat", [(i, i ^ mask) for i in range(owners)])

    def across(values):
        return lax.ppermute(values, "ckpt", [(0, 1), (1, 0)])

    near_own = inputs[0]
    far_own = swap(near_own, 8)
    near = [near_own] + [swap(near_own, place) for place in range(1, 4)]
    partner_bias = swap(enc_bias, 4)
    partner = swap(send_columns(ids, at, enc_weight[0], owners), 4)
    far = [far_own] + [swap(far_own, place) for place in range(1, 4)]

    plane = lat // 4
    rows = []
    for whose, values in ((lat, enc_bias), (lat ^ 4, partner_bias)):
        for index in range(2):
            block = lax.dynamic_slice(block_ids, (plane ^ (2 * index), whose), (1, 1))[0, 0]
            rows.append(lax.dynamic_slice(values, (block * BLOCK,), (BLOCK,)))
    bias = jnp.where(core == 0, jnp.stack(rows), 0.0)
    bias = jnp.broadcast_to(bias[:, :, None], (4, BLOCK, TILE))

    columns = stage_decoder(ids, dec_weight[0], owners, tiles)
    ids_encode, columns = lax.optimization_barrier((ids, columns))
    partial = encode(ids_encode, alive, at, near, far, enc_weight[0], partner, bias, owners)
    acts = jnp.maximum(partial + across(partial), 0.0).astype(BF16).reshape(2, 2, BLOCK, TILE)

    ends = [(2 * i, 2 * (i ^ 4)) for i in range(owners)] + [(2 * i + 1, 2 * (i ^ 12) + 1) for i in range(owners)]
    along = lax.ppermute(acts, ("lat", "ckpt"), ends)
    middle = swap(acts, 8)

    def half(values):
        return lax.dynamic_slice_in_dim(values, core, 1, 0)

    payload = jnp.concatenate([half(acts), along, half(middle)], axis=0)
    mine = [payload] + [swap(payload, place) for place in range(1, 4)]
    theirs = [across(values) for values in mine]
    recon = decode(ids, at, mine, theirs, columns, dec_bias.reshape(-1, 1), owners)
    return recon[None]


def body(inputs, enc_weight, enc_bias, dec_weight, dec_bias, block_ids, live):
    tiles, owners = block_ids.shape
    cores = lax.axis_size("ckpt")
    if owners == 16 and cores == 2 and tiles == 4 and inputs.shape[:2] == (1, tiles * TILE // owners):
        return body_planes(inputs, enc_weight, enc_bias, dec_weight, dec_bias, block_ids, live)
    return body_any(inputs, enc_weight, enc_bias, dec_weight, dec_bias, block_ids, live)


def solution(mesh):
    placed = (
        P("ckpt", ("groups", "lat"), None),
        P("ckpt", None, "lat"),
        P("lat"),
        P("ckpt", "lat", None),
        P("ckpt", "lat"),
        P("groups", None),
        P("groups", None),
    )
    return jax.shard_map(
        body, mesh=mesh, in_specs=placed, out_specs=P("ckpt", "lat", "groups"), check_vma=False
    )
```

```python
import functools

import jax
import jax.numpy as jnp
from jax import lax
from jax.experimental import pallas as pl
from jax.experimental.pallas import tpu as pltpu
from jax.sharding import PartitionSpec as P

BLOCK = 64
TILE = 128
PAIR = 2 * BLOCK
EXTRA = 16
FIRST = 2048
F32 = jnp.float32
BF16 = jnp.bfloat16
VMEM_WEIGHTS = 50 * 1024 * 1024
VMEM_SMALL = 12 * 1024 * 1024


def body_any(inputs, enc_weight, enc_bias, dec_weight, dec_bias, block_ids, live):
    lat_count = lax.axis_size("lat")
    lat_index = lax.axis_index("lat")
    lat_dev = enc_weight.shape[2]
    own_blocks = lat_dev // BLOCK
    local_ckpts = dec_weight.shape[0]
    features = dec_weight.shape[1]
    preact = jnp.einsum(
        "cdl,crd->lr",
        enc_weight,
        lax.all_gather(inputs, "lat", axis=1, tiled=True),
        preferred_element_type=F32,
    )
    token_count = preact.shape[1]
    tiles = token_count // TILE
    own_ids = lax.dynamic_slice_in_dim(block_ids, lat_index, 1, 1)[:, 0]
    own_live = lax.dynamic_slice_in_dim(live, lat_index, 1, 1)[:, 0]
    choose = (own_ids[:, None] == jnp.arange(own_blocks, dtype=jnp.int32)[None, :]) & (own_live[:, None] == 1)
    choose_cols = jnp.transpose(choose.astype(F32))
    grouped_vals = preact.reshape(own_blocks, BLOCK, tiles, TILE)
    picked = jnp.sum(grouped_vals * choose_cols[:, None, :, None], axis=0)
    picked_bias = jnp.einsum("pe,pt->et", enc_bias.reshape(own_blocks, BLOCK), choose_cols, precision=lax.Precision.HIGHEST)
    summed = lax.psum(picked, "ckpt") + picked_bias[:, :, None]
    acts = jnp.transpose(jnp.maximum(summed, 0.0), (1, 0, 2)).astype(BF16)
    onehot = (
        (block_ids[:, :, None] == jnp.arange(own_blocks, dtype=jnp.int32)[None, None, :]) & (live[:, :, None] == 1)
    ).astype(BF16)
    grouped = dec_weight.reshape(local_ckpts, features, lat_count, own_blocks, BLOCK)
    selected = jnp.einsum("tnp,cdnpe->cdtne", onehot, grouped, preferred_element_type=F32).astype(BF16)
    total = jnp.einsum(
        "ntes,cdtne->cdts",
        lax.all_gather(acts[None], "lat", axis=0, tiled=True),
        selected,
        preferred_element_type=F32,
    )
    recon = total.reshape(local_ckpts, features, token_count)
    return (recon + dec_bias[:, :, None]).astype(BF16)


def swap_if(flag, values):
    return jnp.where(flag, pltpu.roll(values, BLOCK, 1), values)


def side_by_side(first, first_odd, second, second_odd):
    lane = lax.broadcasted_iota(jnp.int32, first.shape, 1)
    return jnp.where(lane < BLOCK, swap_if(first_odd == 1, first), swap_if(second_odd == 0, second))


def column_of(block):
    return pl.ds(pl.multiple_of((block // 2) * PAIR, PAIR), PAIR)


SMEM = pl.BlockSpec(memory_space=pltpu.SMEM)
VMEM = pl.BlockSpec(memory_space=pltpu.VMEM)
ANY = pl.BlockSpec(memory_space=pl.ANY)


def params(limit=VMEM_WEIGHTS):
    return pltpu.CompilerParams(vmem_limit_bytes=limit)


def cost(flops, moved):
    return pl.CostEstimate(flops=flops, bytes_accessed=moved, transcendentals=0)


def send_columns_kernel(ids_ref, weight_ref, bias_ref, out_ref, in_ref, sems, *, step, base):
    lat = lax.axis_index("lat")
    plane = lat // 4
    depth = in_ref.shape[1]
    chunks = depth // step
    extra = out_ref.shape[0] - depth
    blocks = [ids_ref[plane ^ mask, lat] for mask in (1, 3)]
    odds = [block % 2 for block in blocks]

    def fetch(chunk, which):
        source = weight_ref.at[pl.ds(base + chunk * step, step), column_of(blocks[which])]
        return pltpu.make_async_copy(source, in_ref.at[which, pl.ds(chunk * step, step)], sems.at[which, chunk])

    for chunk in range(chunks):
        for which in range(2):
            fetch(chunk, which).start()

    if extra:
        parts = [bias_ref[pl.ds(block // 2, 1), :] for block in blocks]
        bias = side_by_side(parts[0], odds[0], parts[1], odds[1])
        high = bias.astype(BF16)
        middle = (bias - high.astype(F32)).astype(BF16)
        low = (bias - high.astype(F32) - middle.astype(F32)).astype(BF16)
        row = lax.broadcasted_iota(jnp.int32, (extra, PAIR), 0)
        rows = jnp.zeros((extra, PAIR), F32)
        for index, part in enumerate((high, middle, low)):
            rows = jnp.where(row == index, jnp.broadcast_to(part.astype(F32), rows.shape), rows)
        out_ref[depth:, :] = rows.astype(BF16)

    for chunk in range(chunks):
        for which in range(2):
            fetch(chunk, which).wait()
        rows = slice(chunk * step, (chunk + 1) * step)
        both = side_by_side(in_ref[0, rows, :].astype(F32), odds[0], in_ref[1, rows, :].astype(F32), odds[1])
        out_ref[rows, :] = both.astype(BF16)


def send_columns(ids, enc_weight, bias, base, depth, extra, step):
    return pl.pallas_call(
        functools.partial(send_columns_kernel, step=step, base=base),
        out_shape=jax.ShapeDtypeStruct((depth + extra, PAIR), BF16),
        in_specs=[SMEM, ANY, VMEM],
        out_specs=VMEM,
        scratch_shapes=[pltpu.VMEM((2, depth, PAIR), BF16), pltpu.SemaphoreType.DMA((2, depth // step))],
        compiler_params=params(),
        cost_estimate=cost(0, 3 * depth * PAIR * 2),
        name="send_columns",
    )(ids, enc_weight, bias)


def own_columns_kernel(ids_ref, weight_ref, out_ref, sems, *, step):
    lat = lax.axis_index("lat")
    copies = []
    for index in range(2):
        lanes = column_of(ids_ref[(lat // 4) ^ (2 * index), lat])
        for chunk in range(out_ref.shape[1] // step):
            rows = pl.ds(chunk * step, step)
            copies.append(
                pltpu.make_async_copy(weight_ref.at[rows, lanes], out_ref.at[index, rows], sems.at[index, chunk])
            )
    for copy in copies:
        copy.start()
    for copy in copies:
        copy.wait()


def own_columns(ids, enc_weight):
    depth = enc_weight.shape[0]
    step = 1024
    return pl.pallas_call(
        functools.partial(own_columns_kernel, step=step),
        out_shape=jax.ShapeDtypeStruct((2, depth, PAIR), BF16),
        in_specs=[SMEM, ANY],
        out_specs=VMEM,
        scratch_shapes=[pltpu.SemaphoreType.DMA((2, depth // step))],
        compiler_params=params(),
        cost_estimate=cost(0, 4 * depth * PAIR * 2),
        name="own_columns",
    )(ids, enc_weight)


def encode_kernel(ids_ref, live_ref, *refs):
    near = refs[0:4]
    far = refs[4:8]
    own_ref, first_ref, rest_ref, bias_ref, out_ref, turn_ref, flip_ref = refs[8:]
    lat, core = lax.axis_index("lat"), lax.axis_index("ckpt")
    plane, place = lat // 4, lat % 4
    depth = own_ref.shape[1]
    shard = TILE // 4
    step = 1024
    parts = first_ref[FIRST:, :].astype(F32)
    other_bias = (parts[0:1] + parts[1:2]) + parts[2:3]
    for index, tokens in enumerate((near, far)):
        total = jnp.zeros((TILE, 2 * PAIR), F32)
        for start in range(0, depth, step):
            rows = jnp.concatenate([ref[:, start : start + step] for ref in tokens], axis=0)
            partner = first_ref[start : start + step, :] if start < FIRST else rest_ref[start - FIRST : start - FIRST + step, :]
            columns = jnp.concatenate([own_ref[index, start : start + step, :], partner], axis=1)
            total += jnp.dot(rows, columns, preferred_element_type=F32)
        tile = plane ^ (2 * index)
        block = ids_ref[tile, lat]
        bias = jnp.concatenate([bias_ref[pl.ds(block // 2, 1), :], other_bias], axis=1)
        total += jnp.where(core == 0, bias, 0.0)
        for turn in range(4):
            to = pl.ds(pl.multiple_of((place ^ turn) * shard, shard), shard)
            turn_ref[to, :] = total[turn * shard : (turn + 1) * shard, :]
        flip_ref[...] = jnp.transpose(turn_ref[:, :PAIR])
        own = flip_ref[pl.ds(pl.multiple_of((block % 2) * BLOCK, BLOCK), BLOCK), :]
        other = jnp.transpose(turn_ref[:, PAIR:])[index * BLOCK : (index + 1) * BLOCK, :]
        out_ref[index] = jnp.where(live_ref[tile, lat] == 1, own, 0.0)
        out_ref[2 + index] = jnp.where(live_ref[tile, lat ^ 4] == 1, other, 0.0)


def encode(ids, live, near, far, own, first, rest, bias):
    return pl.pallas_call(
        encode_kernel,
        out_shape=jax.ShapeDtypeStruct((4, BLOCK, TILE), F32),
        in_specs=[SMEM, SMEM] + [VMEM] * 12,
        out_specs=VMEM,
        scratch_shapes=[pltpu.VMEM((TILE, 2 * PAIR), F32), pltpu.VMEM((PAIR, TILE), F32)],
        compiler_params=params(VMEM_SMALL),
        cost_estimate=cost(4 * TILE * own.shape[1] * 2 * PAIR, 5 * 2**20),
        name="encode",
    )(ids, live, *near, *far, own, first, rest, bias)


def stage_decoder_kernel(ids_ref, weight_ref, out_ref, in_ref, sems):
    tiles, owners = ids_ref.shape
    span = weight_ref.shape[1] // owners

    def fetch(tile, owner):
        lanes = pl.ds(pl.multiple_of(owner * span + (ids_ref[tile, owner] // 2) * PAIR, PAIR), PAIR)
        return pltpu.make_async_copy(weight_ref.at[:, lanes], in_ref.at[tile, owner], sems.at[tile, owner])

    for tile in range(tiles):
        for owner in range(owners):
            fetch(tile, owner).start()
    for tile in range(tiles):
        for owner in range(0, owners, 2):
            fetch(tile, owner).wait()
            fetch(tile, owner + 1).wait()
            both = side_by_side(
                in_ref[tile, owner].astype(F32),
                ids_ref[tile, owner] % 2,
                in_ref[tile, owner + 1].astype(F32),
                ids_ref[tile, owner + 1] % 2,
            )
            out_ref[tile, :, owner * BLOCK : owner * BLOCK + PAIR] = both.astype(BF16)


def stage_decoder(ids, dec_weight):
    tiles, owners = ids.shape
    features = dec_weight.shape[0]
    return pl.pallas_call(
        stage_decoder_kernel,
        out_shape=jax.ShapeDtypeStruct((tiles, features, owners * BLOCK), BF16),
        in_specs=[SMEM, ANY],
        out_specs=VMEM,
        scratch_shapes=[
            pltpu.VMEM((tiles, owners, features, PAIR), BF16),
            pltpu.SemaphoreType.DMA((tiles, owners)),
        ],
        compiler_params=params(),
        cost_estimate=cost(0, 6 * tiles * features * owners * BLOCK),
        name="stage_decoder",
    )(ids, dec_weight)


def decode_kernel(*refs):
    mine = refs[0:4]
    theirs = refs[4:8]
    columns_ref, bias_ref, out_ref, acts_ref, back_ref, sems = refs[8:]
    lat, core = lax.axis_index("lat"), lax.axis_index("ckpt")
    tiles, _, depth = columns_ref.shape
    for place in range(4):
        for ref, holder in ((mine[place], core), (theirs[place], 1 - core)):
            slots = ((0, holder), (4 + 8 * holder, 0), (4 + 8 * holder, 1), (8, holder))
            for slot, (mask, which) in enumerate(slots):
                source = lat ^ place ^ mask
                owner = source ^ (4 * which)
                for index in range(2):
                    tile = (source // 4) ^ (2 * index)
                    row = pl.multiple_of(tile * depth + owner * BLOCK, BLOCK)
                    acts_ref[pl.ds(row, BLOCK), :] = ref[slot, index]

    def give(tile):
        lanes = pl.ds(tile * TILE, TILE)
        return pltpu.make_async_copy(back_ref.at[tile], out_ref.at[:, lanes], sems.at[tile])

    for tile in range(tiles):
        acts = acts_ref[tile * depth : (tile + 1) * depth, :]
        total = jnp.dot(columns_ref[tile], acts, preferred_element_type=F32)
        back_ref[tile] = (total + bias_ref[...]).astype(BF16)
        give(tile).start()
    for tile in range(tiles):
        give(tile).wait()


def decode(mine, theirs, columns, dec_bias):
    tiles, features, depth = columns.shape
    return pl.pallas_call(
        decode_kernel,
        out_shape=jax.ShapeDtypeStruct((features, tiles * TILE), BF16),
        in_specs=[VMEM] * 10,
        out_specs=ANY,
        scratch_shapes=[
            pltpu.VMEM((tiles * depth, TILE), BF16),
            pltpu.VMEM((tiles, features, TILE), BF16),
            pltpu.SemaphoreType.DMA((tiles,)),
        ],
        compiler_params=params(VMEM_SMALL),
        cost_estimate=cost(2 * tiles * features * depth * TILE, 4 * 2**20),
        name="decode",
    )(*mine, *theirs, columns, dec_bias)


def body_planes(inputs, enc_weight, enc_bias, dec_weight, dec_bias, block_ids, live):
    owners = lax.axis_size("lat")
    core = lax.axis_index("ckpt")

    def swap(values, mask):
        return lax.ppermute(values, "lat", [(i, i ^ mask) for i in range(owners)])

    def across(values):
        return lax.ppermute(values, "ckpt", [(0, 1), (1, 0)])

    near_own = inputs[0]
    far_own = swap(near_own, 8)
    near = [near_own] + [swap(near_own, place) for place in range(1, 4)]
    bias = enc_bias.reshape(-1, PAIR)
    first = swap(send_columns(block_ids, enc_weight[0], bias, 0, FIRST, EXTRA, 512), 4)
    depth = enc_weight.shape[1]
    rest = send_columns(block_ids, enc_weight[0], bias, FIRST, depth - FIRST, 0, 512)
    rest = swap(rest, 4)
    own = own_columns(block_ids, enc_weight[0])
    near[1], near[2], near[3], far_own, own = lax.optimization_barrier((near[1], near[2], near[3], far_own, own))
    columns = stage_decoder(block_ids, dec_weight[0])
    far = [far_own] + [swap(far_own, place) for place in range(1, 4)]

    partial = encode(block_ids, live, near, far, own, first, rest, bias)
    partial, columns = lax.optimization_barrier((partial, columns))
    acts = jnp.maximum(partial + across(partial), 0.0).astype(BF16).reshape(2, 2, BLOCK, TILE)

    ends = [(2 * i, 2 * (i ^ 4)) for i in range(owners)] + [(2 * i + 1, 2 * (i ^ 12) + 1) for i in range(owners)]
    along = lax.ppermute(acts, ("lat", "ckpt"), ends)
    middle = swap(acts, 8)

    def half(values):
        return lax.dynamic_slice_in_dim(values, core, 1, 0)

    payload = jnp.concatenate([half(acts), along, half(middle)], axis=0)
    mine = [payload] + [swap(payload, place) for place in range(1, 4)]
    theirs = [across(values) for values in mine]
    recon = decode(mine, theirs, columns, dec_bias.reshape(-1, 1))
    return recon[None]


def body(inputs, enc_weight, enc_bias, dec_weight, dec_bias, block_ids, live):
    tiles, owners = block_ids.shape
    cores = lax.axis_size("ckpt")
    if owners == 16 and cores == 2 and tiles == 4 and inputs.shape[:2] == (1, tiles * TILE // owners):
        return body_planes(inputs, enc_weight, enc_bias, dec_weight, dec_bias, block_ids, live)
    return body_any(inputs, enc_weight, enc_bias, dec_weight, dec_bias, block_ids, live)


def solution(mesh):
    placed = (
        P("ckpt", ("groups", "lat"), None),
        P("ckpt", None, "lat"),
        P("lat"),
        P("ckpt", "lat", None),
        P("ckpt", "lat"),
        P("groups", None),
        P("groups", None),
    )
    return jax.shard_map(
        body, mesh=mesh, in_specs=placed, out_specs=P("ckpt", "lat", "groups"), check_vma=False
    )
```

```python
import functools

import jax
import jax.numpy as jnp
from jax import lax
from jax.experimental import pallas as pl
from jax.experimental.pallas import tpu as pltpu
from jax.sharding import PartitionSpec as P

BLOCK = 64
TILE = 128
PAIR = 2 * BLOCK
EXTRA = 16
FIRST = 1024
F32 = jnp.float32
BF16 = jnp.bfloat16
VMEM_WEIGHTS = 50 * 1024 * 1024
VMEM_SMALL = 12 * 1024 * 1024


def body_any(inputs, enc_weight, enc_bias, dec_weight, dec_bias, block_ids, live):
    lat_count = lax.axis_size("lat")
    lat_index = lax.axis_index("lat")
    lat_dev = enc_weight.shape[2]
    own_blocks = lat_dev // BLOCK
    local_ckpts = dec_weight.shape[0]
    features = dec_weight.shape[1]
    preact = jnp.einsum(
        "cdl,crd->lr",
        enc_weight,
        lax.all_gather(inputs, "lat", axis=1, tiled=True),
        preferred_element_type=F32,
    )
    token_count = preact.shape[1]
    tiles = token_count // TILE
    own_ids = lax.dynamic_slice_in_dim(block_ids, lat_index, 1, 1)[:, 0]
    own_live = lax.dynamic_slice_in_dim(live, lat_index, 1, 1)[:, 0]
    choose = (own_ids[:, None] == jnp.arange(own_blocks, dtype=jnp.int32)[None, :]) & (own_live[:, None] == 1)
    choose_cols = jnp.transpose(choose.astype(F32))
    grouped_vals = preact.reshape(own_blocks, BLOCK, tiles, TILE)
    picked = jnp.sum(grouped_vals * choose_cols[:, None, :, None], axis=0)
    picked_bias = jnp.einsum("pe,pt->et", enc_bias.reshape(own_blocks, BLOCK), choose_cols, precision=lax.Precision.HIGHEST)
    summed = lax.psum(picked, "ckpt") + picked_bias[:, :, None]
    acts = jnp.transpose(jnp.maximum(summed, 0.0), (1, 0, 2)).astype(BF16)
    onehot = (
        (block_ids[:, :, None] == jnp.arange(own_blocks, dtype=jnp.int32)[None, None, :]) & (live[:, :, None] == 1)
    ).astype(BF16)
    grouped = dec_weight.reshape(local_ckpts, features, lat_count, own_blocks, BLOCK)
    selected = jnp.einsum("tnp,cdnpe->cdtne", onehot, grouped, preferred_element_type=F32).astype(BF16)
    total = jnp.einsum(
        "ntes,cdtne->cdts",
        lax.all_gather(acts[None], "lat", axis=0, tiled=True),
        selected,
        preferred_element_type=F32,
    )
    recon = total.reshape(local_ckpts, features, token_count)
    return (recon + dec_bias[:, :, None]).astype(BF16)


def swap_if(flag, values):
    return jnp.where(flag, pltpu.roll(values, BLOCK, 1), values)


def side_by_side(first, first_odd, second, second_odd):
    lane = lax.broadcasted_iota(jnp.int32, first.shape, 1)
    return jnp.where(lane < BLOCK, swap_if(first_odd == 1, first), swap_if(second_odd == 0, second))


def column_of(block):
    return pl.ds(pl.multiple_of((block // 2) * PAIR, PAIR), PAIR)


SMEM = pl.BlockSpec(memory_space=pltpu.SMEM)
VMEM = pl.BlockSpec(memory_space=pltpu.VMEM)
ANY = pl.BlockSpec(memory_space=pl.ANY)


def params(limit=VMEM_WEIGHTS):
    return pltpu.CompilerParams(vmem_limit_bytes=limit)


def cost(flops, moved):
    return pl.CostEstimate(flops=flops, bytes_accessed=moved, transcendentals=0)


def send_columns_kernel(ids_ref, weight_ref, *refs, step, base):
    *bias_refs, out_ref, in_ref, sems = refs
    lat = lax.axis_index("lat")
    plane = lat // 4
    depth = in_ref.shape[1]
    chunks = depth // step
    folded = out_ref.shape[1] > PAIR
    blocks = [ids_ref[plane ^ mask, lat] for mask in (1, 3)]
    odds = [block % 2 for block in blocks]

    def fetch(chunk, which):
        source = weight_ref.at[pl.ds(base + chunk * step, step), column_of(blocks[which])]
        return pltpu.make_async_copy(source, in_ref.at[which, pl.ds(chunk * step, step)], sems.at[which, chunk])

    for chunk in range(chunks):
        for which in range(2):
            fetch(chunk, which).start()

    if bias_refs:
        (bias_ref,) = bias_refs
        extra = out_ref.shape[0] - depth
        parts = [bias_ref[pl.ds(block // 2, 1), :] for block in blocks]
        bias = side_by_side(parts[0], odds[0], parts[1], odds[1])
        high = bias.astype(BF16)
        middle = (bias - high.astype(F32)).astype(BF16)
        low = (bias - high.astype(F32) - middle.astype(F32)).astype(BF16)
        row = lax.broadcasted_iota(jnp.int32, (extra, PAIR), 0)
        rows = jnp.zeros((extra, PAIR), F32)
        for index, part in enumerate((high, middle, low)):
            rows = jnp.where(row == index, jnp.broadcast_to(part.astype(F32), rows.shape), rows)
        out_ref[depth:, :] = rows.astype(BF16)

    for chunk in range(chunks):
        for which in range(2):
            fetch(chunk, which).wait()
        rows = slice(chunk * step, (chunk + 1) * step)
        both = side_by_side(in_ref[0, rows, :].astype(F32), odds[0], in_ref[1, rows, :].astype(F32), odds[1])
        both = both.astype(BF16)
        if folded:
            high = out_ref.shape[0]
            for piece in range(step // high):
                left = (chunk * (step // high) + piece) * PAIR
                out_ref[:, left : left + PAIR] = both[piece * high : (piece + 1) * high, :]
        else:
            out_ref[rows, :] = both


def send_columns(ids, enc_weight, bias, base, depth, shape, step):
    return pl.pallas_call(
        functools.partial(send_columns_kernel, step=step, base=base),
        out_shape=jax.ShapeDtypeStruct(shape, BF16),
        in_specs=[SMEM, ANY] + [VMEM] * len(bias),
        out_specs=VMEM,
        scratch_shapes=[pltpu.VMEM((2, depth, PAIR), BF16), pltpu.SemaphoreType.DMA((2, depth // step))],
        compiler_params=params(),
        cost_estimate=cost(0, 3 * depth * PAIR * 2),
        name="send_columns",
    )(ids, enc_weight, *bias)


def own_columns_kernel(ids_ref, weight_ref, out_ref, sems, *, step):
    lat = lax.axis_index("lat")
    copies = []
    for index in range(2):
        lanes = column_of(ids_ref[(lat // 4) ^ (2 * index), lat])
        for chunk in range(out_ref.shape[1] // step):
            rows = pl.ds(chunk * step, step)
            copies.append(
                pltpu.make_async_copy(weight_ref.at[rows, lanes], out_ref.at[index, rows], sems.at[index, chunk])
            )
    for copy in copies:
        copy.start()
    for copy in copies:
        copy.wait()


def own_columns(ids, enc_weight):
    depth = enc_weight.shape[0]
    step = 1024
    return pl.pallas_call(
        functools.partial(own_columns_kernel, step=step),
        out_shape=jax.ShapeDtypeStruct((2, depth, PAIR), BF16),
        in_specs=[SMEM, ANY],
        out_specs=VMEM,
        scratch_shapes=[pltpu.SemaphoreType.DMA((2, depth // step))],
        compiler_params=params(),
        cost_estimate=cost(0, 4 * depth * PAIR * 2),
        name="own_columns",
    )(ids, enc_weight)


def encode_kernel(ids_ref, live_ref, *refs):
    near = refs[0:4]
    far = refs[4:8]
    own_ref, first_ref, rest_ref, bias_ref, out_ref, turn_ref, flip_ref = refs[8:]
    lat, core = lax.axis_index("lat"), lax.axis_index("ckpt")
    plane, place = lat // 4, lat % 4
    depth = own_ref.shape[1]
    shard = TILE // 4
    step = 1024
    parts = rest_ref[depth - FIRST :, :].astype(F32)
    other_bias = (parts[0:1] + parts[1:2]) + parts[2:3]
    for index, tokens in enumerate((near, far)):
        total = jnp.zeros((TILE, 2 * PAIR), F32)
        for start in range(0, depth, step):
            rows = jnp.concatenate([ref[:, start : start + step] for ref in tokens], axis=0)
            if start < FIRST:
                pieces = range(start // shard, (start + step) // shard)
                partner = jnp.concatenate([first_ref[:, i * PAIR : (i + 1) * PAIR] for i in pieces], axis=0)
            else:
                partner = rest_ref[start - FIRST : start - FIRST + step, :]
            columns = jnp.concatenate([own_ref[index, start : start + step, :], partner], axis=1)
            total += jnp.dot(rows, columns, preferred_element_type=F32)
        tile = plane ^ (2 * index)
        block = ids_ref[tile, lat]
        bias = jnp.concatenate([bias_ref[pl.ds(block // 2, 1), :], other_bias], axis=1)
        total += jnp.where(core == 0, bias, 0.0)
        for turn in range(4):
            to = pl.ds(pl.multiple_of((place ^ turn) * shard, shard), shard)
            turn_ref[to, :] = total[turn * shard : (turn + 1) * shard, :]
        flip_ref[...] = jnp.transpose(turn_ref[:, :PAIR])
        own = flip_ref[pl.ds(pl.multiple_of((block % 2) * BLOCK, BLOCK), BLOCK), :]
        other = jnp.transpose(turn_ref[:, PAIR:])[index * BLOCK : (index + 1) * BLOCK, :]
        out_ref[index] = jnp.where(live_ref[tile, lat] == 1, own, 0.0)
        out_ref[2 + index] = jnp.where(live_ref[tile, lat ^ 4] == 1, other, 0.0)


def encode(ids, live, near, far, own, first, rest, bias):
    return pl.pallas_call(
        encode_kernel,
        out_shape=jax.ShapeDtypeStruct((4, BLOCK, TILE), F32),
        in_specs=[SMEM, SMEM] + [VMEM] * 12,
        out_specs=VMEM,
        scratch_shapes=[pltpu.VMEM((TILE, 2 * PAIR), F32), pltpu.VMEM((PAIR, TILE), F32)],
        compiler_params=params(VMEM_SMALL),
        cost_estimate=cost(4 * TILE * own.shape[1] * 2 * PAIR, 5 * 2**20),
        name="encode",
    )(ids, live, *near, *far, own, first, rest, bias)


def stage_decoder_kernel(ids_ref, weight_ref, out_ref, in_ref, sems):
    tiles, owners = ids_ref.shape
    span = weight_ref.shape[1] // owners

    def fetch(tile, owner):
        lanes = pl.ds(pl.multiple_of(owner * span + (ids_ref[tile, owner] // 2) * PAIR, PAIR), PAIR)
        return pltpu.make_async_copy(weight_ref.at[:, lanes], in_ref.at[tile, owner], sems.at[tile, owner])

    for tile in range(tiles):
        for owner in range(owners):
            fetch(tile, owner).start()
    for tile in range(tiles):
        for owner in range(0, owners, 2):
            fetch(tile, owner).wait()
            fetch(tile, owner + 1).wait()
            both = side_by_side(
                in_ref[tile, owner].astype(F32),
                ids_ref[tile, owner] % 2,
                in_ref[tile, owner + 1].astype(F32),
                ids_ref[tile, owner + 1] % 2,
            )
            out_ref[tile, :, owner * BLOCK : owner * BLOCK + PAIR] = both.astype(BF16)


def stage_decoder(ids, dec_weight):
    tiles, owners = ids.shape
    features = dec_weight.shape[0]
    return pl.pallas_call(
        stage_decoder_kernel,
        out_shape=jax.ShapeDtypeStruct((tiles, features, owners * BLOCK), BF16),
        in_specs=[SMEM, ANY],
        out_specs=VMEM,
        scratch_shapes=[
            pltpu.VMEM((tiles, owners, features, PAIR), BF16),
            pltpu.SemaphoreType.DMA((tiles, owners)),
        ],
        compiler_params=params(),
        cost_estimate=cost(0, 6 * tiles * features * owners * BLOCK),
        name="stage_decoder",
    )(ids, dec_weight)


def decode_kernel(*refs):
    mine = refs[0:4]
    theirs = refs[4:8]
    columns_ref, bias_ref, out_ref, acts_ref, back_ref, sems = refs[8:]
    lat, core = lax.axis_index("lat"), lax.axis_index("ckpt")
    tiles, _, depth = columns_ref.shape
    for place in range(4):
        for ref, holder in ((mine[place], core), (theirs[place], 1 - core)):
            slots = ((0, holder), (4 + 8 * holder, 0), (4 + 8 * holder, 1), (8, holder))
            for slot, (mask, which) in enumerate(slots):
                source = lat ^ place ^ mask
                owner = source ^ (4 * which)
                for index in range(2):
                    tile = (source // 4) ^ (2 * index)
                    row = pl.multiple_of(tile * depth + owner * BLOCK, BLOCK)
                    acts_ref[pl.ds(row, BLOCK), :] = ref[slot, index]

    def give(tile):
        lanes = pl.ds(tile * TILE, TILE)
        return pltpu.make_async_copy(back_ref.at[tile], out_ref.at[:, lanes], sems.at[tile])

    for tile in range(tiles):
        acts = acts_ref[tile * depth : (tile + 1) * depth, :]
        total = jnp.dot(columns_ref[tile], acts, preferred_element_type=F32)
        back_ref[tile] = (total + bias_ref[...]).astype(BF16)
        give(tile).start()
    for tile in range(tiles):
        give(tile).wait()


def decode(mine, theirs, columns, dec_bias):
    tiles, features, depth = columns.shape
    return pl.pallas_call(
        decode_kernel,
        out_shape=jax.ShapeDtypeStruct((features, tiles * TILE), BF16),
        in_specs=[VMEM] * 10,
        out_specs=ANY,
        scratch_shapes=[
            pltpu.VMEM((tiles * depth, TILE), BF16),
            pltpu.VMEM((tiles, features, TILE), BF16),
            pltpu.SemaphoreType.DMA((tiles,)),
        ],
        compiler_params=params(VMEM_SMALL),
        cost_estimate=cost(2 * tiles * features * depth * TILE, 4 * 2**20),
        name="decode",
    )(*mine, *theirs, columns, dec_bias)


def body_planes(inputs, enc_weight, enc_bias, dec_weight, dec_bias, block_ids, live):
    owners = lax.axis_size("lat")
    core = lax.axis_index("ckpt")

    def swap(values, mask):
        return lax.ppermute(values, "lat", [(i, i ^ mask) for i in range(owners)])

    def across(values):
        return lax.ppermute(values, "ckpt", [(0, 1), (1, 0)])

    near_own = inputs[0]
    near = [near_own] + [swap(near_own, place) for place in range(1, 4)]
    bias = enc_bias.reshape(-1, PAIR)
    depth = enc_weight.shape[1]
    first = send_columns(block_ids, enc_weight[0], [], 0, FIRST, near_own.shape, 256)
    plane = lax.axis_index("lat") // 4
    at_end = (plane == 0) | (plane == 3)

    def rotate(values, end_mask, middle_mask):
        pairs = [(i, i ^ (end_mask if i // 4 in (0, 3) else middle_mask)) for i in range(owners)]
        return lax.ppermute(values, "lat", pairs)

    one = rotate(jnp.where(at_end, first, near_own), 4, 8)
    two = rotate(jnp.where(at_end, near_own, first), 8, 4)
    rest = send_columns(block_ids, enc_weight[0], [bias], FIRST, depth - FIRST, (depth - FIRST + EXTRA, PAIR), 512)
    rest, one = lax.optimization_barrier((rest, one))
    rest = swap(rest, 4)
    far_own = jnp.where(at_end, one, two)
    first = jnp.where(at_end, two, one)
    own = own_columns(block_ids, enc_weight[0])
    far_own, own = lax.optimization_barrier((far_own, own))
    columns = stage_decoder(block_ids, dec_weight[0])
    far = [far_own] + [swap(far_own, place) for place in range(1, 4)]

    partial = encode(block_ids, live, near, far, own, first, rest, bias)
    partial, columns = lax.optimization_barrier((partial, columns))
    acts = jnp.maximum(partial + across(partial), 0.0).astype(BF16).reshape(2, 2, BLOCK, TILE)

    ends = [(2 * i, 2 * (i ^ 4)) for i in range(owners)] + [(2 * i + 1, 2 * (i ^ 12) + 1) for i in range(owners)]
    along = lax.ppermute(acts, ("lat", "ckpt"), ends)
    mine_half = lax.dynamic_slice_in_dim(acts, core, 1, 0)
    middle = swap(mine_half, 8)
    payload = jnp.concatenate([mine_half, along, middle], axis=0)
    mine = [payload] + [swap(payload, place) for place in range(1, 4)]
    theirs = [across(values) for values in mine]
    recon = decode(mine, theirs, columns, dec_bias.reshape(-1, 1))
    return recon[None]


def body(inputs, enc_weight, enc_bias, dec_weight, dec_bias, block_ids, live):
    tiles, owners = block_ids.shape
    cores = lax.axis_size("ckpt")
    if owners == 16 and cores == 2 and tiles == 4 and inputs.shape[:2] == (1, tiles * TILE // owners):
        return body_planes(inputs, enc_weight, enc_bias, dec_weight, dec_bias, block_ids, live)
    return body_any(inputs, enc_weight, enc_bias, dec_weight, dec_bias, block_ids, live)


def solution(mesh):
    placed = (
        P("ckpt", ("groups", "lat"), None),
        P("ckpt", None, "lat"),
        P("lat"),
        P("ckpt", "lat", None),
        P("ckpt", "lat"),
        P("groups", None),
        P("groups", None),
    )
    return jax.shard_map(
        body, mesh=mesh, in_specs=placed, out_specs=P("ckpt", "lat", "groups"), check_vma=False
    )
```

```python
import functools

import jax
import jax.numpy as jnp
from jax import lax
from jax.experimental import pallas as pl
from jax.experimental.pallas import tpu as pltpu
from jax.sharding import PartitionSpec as P

BLOCK = 64
TILE = 128
PAIR = 2 * BLOCK
EXTRA = 16
FIRST = 1024
F32 = jnp.float32
BF16 = jnp.bfloat16
VMEM_WEIGHTS = 50 * 1024 * 1024
VMEM_SMALL = 12 * 1024 * 1024


def body_any(inputs, enc_weight, enc_bias, dec_weight, dec_bias, block_ids, live):
    lat_count = lax.axis_size("lat")
    lat_index = lax.axis_index("lat")
    lat_dev = enc_weight.shape[2]
    own_blocks = lat_dev // BLOCK
    local_ckpts = dec_weight.shape[0]
    features = dec_weight.shape[1]
    preact = jnp.einsum(
        "cdl,crd->lr",
        enc_weight,
        lax.all_gather(inputs, "lat", axis=1, tiled=True),
        preferred_element_type=F32,
    )
    token_count = preact.shape[1]
    tiles = token_count // TILE
    own_ids = lax.dynamic_slice_in_dim(block_ids, lat_index, 1, 1)[:, 0]
    own_live = lax.dynamic_slice_in_dim(live, lat_index, 1, 1)[:, 0]
    choose = (own_ids[:, None] == jnp.arange(own_blocks, dtype=jnp.int32)[None, :]) & (own_live[:, None] == 1)
    choose_cols = jnp.transpose(choose.astype(F32))
    grouped_vals = preact.reshape(own_blocks, BLOCK, tiles, TILE)
    picked = jnp.sum(grouped_vals * choose_cols[:, None, :, None], axis=0)
    picked_bias = jnp.einsum("pe,pt->et", enc_bias.reshape(own_blocks, BLOCK), choose_cols, precision=lax.Precision.HIGHEST)
    summed = lax.psum(picked, "ckpt") + picked_bias[:, :, None]
    acts = jnp.transpose(jnp.maximum(summed, 0.0), (1, 0, 2)).astype(BF16)
    onehot = (
        (block_ids[:, :, None] == jnp.arange(own_blocks, dtype=jnp.int32)[None, None, :]) & (live[:, :, None] == 1)
    ).astype(BF16)
    grouped = dec_weight.reshape(local_ckpts, features, lat_count, own_blocks, BLOCK)
    selected = jnp.einsum("tnp,cdnpe->cdtne", onehot, grouped, preferred_element_type=F32).astype(BF16)
    total = jnp.einsum(
        "ntes,cdtne->cdts",
        lax.all_gather(acts[None], "lat", axis=0, tiled=True),
        selected,
        preferred_element_type=F32,
    )
    recon = total.reshape(local_ckpts, features, token_count)
    return (recon + dec_bias[:, :, None]).astype(BF16)


def swap_if(flag, values):
    return jnp.where(flag, pltpu.roll(values, BLOCK, 1), values)


def side_by_side(first, first_odd, second, second_odd):
    lane = lax.broadcasted_iota(jnp.int32, first.shape, 1)
    return jnp.where(lane < BLOCK, swap_if(first_odd == 1, first), swap_if(second_odd == 0, second))


def column_of(block):
    return pl.ds(pl.multiple_of((block // 2) * PAIR, PAIR), PAIR)


SMEM = pl.BlockSpec(memory_space=pltpu.SMEM)
VMEM = pl.BlockSpec(memory_space=pltpu.VMEM)
ANY = pl.BlockSpec(memory_space=pl.ANY)


def params(limit=VMEM_WEIGHTS):
    return pltpu.CompilerParams(vmem_limit_bytes=limit)


def cost(flops, moved):
    return pl.CostEstimate(flops=flops, bytes_accessed=moved, transcendentals=0)


def send_columns_kernel(all_ids_ref, weight_ref, *refs, step, base):
    *bias_refs, out_ref, in_ref, ids_ref, ids_sem, sems = refs
    ids_copy = pltpu.make_async_copy(all_ids_ref, ids_ref, ids_sem)
    ids_copy.start()
    ids_copy.wait()
    lat = lax.axis_index("lat")
    plane = lat // 4
    depth = in_ref.shape[1]
    chunks = depth // step
    folded = out_ref.shape[1] > PAIR
    blocks = [ids_ref[plane ^ mask, lat] for mask in (1, 3)]
    odds = [block % 2 for block in blocks]

    def fetch(chunk, which):
        source = weight_ref.at[pl.ds(base + chunk * step, step), column_of(blocks[which])]
        return pltpu.make_async_copy(source, in_ref.at[which, pl.ds(chunk * step, step)], sems.at[which, chunk])

    for chunk in range(chunks):
        for which in range(2):
            fetch(chunk, which).start()

    if bias_refs:
        (bias_ref,) = bias_refs
        extra = out_ref.shape[0] - depth
        parts = [bias_ref[pl.ds(block // 2, 1), :] for block in blocks]
        bias = side_by_side(parts[0], odds[0], parts[1], odds[1])
        high = bias.astype(BF16)
        middle = (bias - high.astype(F32)).astype(BF16)
        low = (bias - high.astype(F32) - middle.astype(F32)).astype(BF16)
        row = lax.broadcasted_iota(jnp.int32, (extra, PAIR), 0)
        rows = jnp.zeros((extra, PAIR), F32)
        for index, part in enumerate((high, middle, low)):
            rows = jnp.where(row == index, jnp.broadcast_to(part.astype(F32), rows.shape), rows)
        out_ref[depth:, :] = rows.astype(BF16)

    for chunk in range(chunks):
        for which in range(2):
            fetch(chunk, which).wait()
        rows = slice(chunk * step, (chunk + 1) * step)
        both = side_by_side(in_ref[0, rows, :].astype(F32), odds[0], in_ref[1, rows, :].astype(F32), odds[1])
        both = both.astype(BF16)
        if folded:
            high = out_ref.shape[0]
            for piece in range(step // high):
                left = (chunk * (step // high) + piece) * PAIR
                out_ref[:, left : left + PAIR] = both[piece * high : (piece + 1) * high, :]
        else:
            out_ref[rows, :] = both


def send_columns(ids, enc_weight, bias, base, depth, shape, step):
    return pl.pallas_call(
        functools.partial(send_columns_kernel, step=step, base=base),
        out_shape=jax.ShapeDtypeStruct(shape, BF16),
        in_specs=[ANY, ANY] + [VMEM] * len(bias),
        out_specs=VMEM,
        scratch_shapes=[
            pltpu.VMEM((2, depth, PAIR), BF16),
            pltpu.SMEM(ids.shape, jnp.int32),
            pltpu.SemaphoreType.DMA,
            pltpu.SemaphoreType.DMA((2, depth // step)),
        ],
        compiler_params=params(),
        cost_estimate=cost(0, 3 * depth * PAIR * 2),
        name="send_columns",
    )(ids, enc_weight, *bias)


def own_columns_kernel(ids_ref, weight_ref, out_ref, sems, *, step):
    lat = lax.axis_index("lat")
    copies = []
    for index in range(2):
        lanes = column_of(ids_ref[(lat // 4) ^ (2 * index), lat])
        for chunk in range(out_ref.shape[1] // step):
            rows = pl.ds(chunk * step, step)
            copies.append(
                pltpu.make_async_copy(weight_ref.at[rows, lanes], out_ref.at[index, rows], sems.at[index, chunk])
            )
    for copy in copies:
        copy.start()
    for copy in copies:
        copy.wait()


def own_columns(ids, enc_weight):
    depth = enc_weight.shape[0]
    step = 1024
    return pl.pallas_call(
        functools.partial(own_columns_kernel, step=step),
        out_shape=jax.ShapeDtypeStruct((2, depth, PAIR), BF16),
        in_specs=[SMEM, ANY],
        out_specs=VMEM,
        scratch_shapes=[pltpu.SemaphoreType.DMA((2, depth // step))],
        compiler_params=params(),
        cost_estimate=cost(0, 4 * depth * PAIR * 2),
        name="own_columns",
    )(ids, enc_weight)


def encode_kernel(ids_ref, live_ref, *refs):
    near = refs[0:4]
    far = refs[4:8]
    own_ref, first_ref, rest_ref, bias_ref, out_ref, turn_ref, flip_ref = refs[8:]
    lat, core = lax.axis_index("lat"), lax.axis_index("ckpt")
    plane, place = lat // 4, lat % 4
    depth = own_ref.shape[1]
    shard = TILE // 4
    step = 1024
    parts = rest_ref[depth - FIRST :, :].astype(F32)
    other_bias = (parts[0:1] + parts[1:2]) + parts[2:3]
    for index, tokens in enumerate((near, far)):
        total = jnp.zeros((TILE, 2 * PAIR), F32)
        for start in range(0, depth, step):
            rows = jnp.concatenate([ref[:, start : start + step] for ref in tokens], axis=0)
            if start < FIRST:
                pieces = range(start // shard, (start + step) // shard)
                partner = jnp.concatenate([first_ref[:, i * PAIR : (i + 1) * PAIR] for i in pieces], axis=0)
            else:
                partner = rest_ref[start - FIRST : start - FIRST + step, :]
            columns = jnp.concatenate([own_ref[index, start : start + step, :], partner], axis=1)
            total += jnp.dot(rows, columns, preferred_element_type=F32)
        tile = plane ^ (2 * index)
        block = ids_ref[tile, lat]
        bias = jnp.concatenate([bias_ref[pl.ds(block // 2, 1), :], other_bias], axis=1)
        total += jnp.where(core == 0, bias, 0.0)
        for turn in range(4):
            to = pl.ds(pl.multiple_of((place ^ turn) * shard, shard), shard)
            turn_ref[to, :] = total[turn * shard : (turn + 1) * shard, :]
        flip_ref[...] = jnp.transpose(turn_ref[:, :PAIR])
        own = flip_ref[pl.ds(pl.multiple_of((block % 2) * BLOCK, BLOCK), BLOCK), :]
        other = jnp.transpose(turn_ref[:, PAIR:])[index * BLOCK : (index + 1) * BLOCK, :]
        out_ref[index] = jnp.where(live_ref[tile, lat] == 1, own, 0.0)
        out_ref[2 + index] = jnp.where(live_ref[tile, lat ^ 4] == 1, other, 0.0)


def encode(ids, live, near, far, own, first, rest, bias):
    return pl.pallas_call(
        encode_kernel,
        out_shape=jax.ShapeDtypeStruct((4, BLOCK, TILE), F32),
        in_specs=[SMEM, SMEM] + [VMEM] * 12,
        out_specs=VMEM,
        scratch_shapes=[pltpu.VMEM((TILE, 2 * PAIR), F32), pltpu.VMEM((PAIR, TILE), F32)],
        compiler_params=params(VMEM_SMALL),
        cost_estimate=cost(4 * TILE * own.shape[1] * 2 * PAIR, 5 * 2**20),
        name="encode",
    )(ids, live, *near, *far, own, first, rest, bias)


def stage_decoder_kernel(ids_ref, weight_ref, out_ref, in_ref, sems):
    tiles, owners = ids_ref.shape
    span = weight_ref.shape[1] // owners

    def fetch(tile, owner):
        lanes = pl.ds(pl.multiple_of(owner * span + (ids_ref[tile, owner] // 2) * PAIR, PAIR), PAIR)
        return pltpu.make_async_copy(weight_ref.at[:, lanes], in_ref.at[tile, owner], sems.at[tile, owner])

    for tile in range(tiles):
        for owner in range(owners):
            fetch(tile, owner).start()
    for tile in range(tiles):
        for owner in range(0, owners, 2):
            fetch(tile, owner).wait()
            fetch(tile, owner + 1).wait()
            both = side_by_side(
                in_ref[tile, owner].astype(F32),
                ids_ref[tile, owner] % 2,
                in_ref[tile, owner + 1].astype(F32),
                ids_ref[tile, owner + 1] % 2,
            )
            out_ref[tile, :, owner * BLOCK : owner * BLOCK + PAIR] = both.astype(BF16)


def stage_decoder(ids, dec_weight):
    tiles, owners = ids.shape
    features = dec_weight.shape[0]
    return pl.pallas_call(
        stage_decoder_kernel,
        out_shape=jax.ShapeDtypeStruct((tiles, features, owners * BLOCK), BF16),
        in_specs=[SMEM, ANY],
        out_specs=VMEM,
        scratch_shapes=[
            pltpu.VMEM((tiles, owners, features, PAIR), BF16),
            pltpu.SemaphoreType.DMA((tiles, owners)),
        ],
        compiler_params=params(),
        cost_estimate=cost(0, 6 * tiles * features * owners * BLOCK),
        name="stage_decoder",
    )(ids, dec_weight)


def decode_kernel(*refs):
    mine = refs[0:4]
    theirs = refs[4:8]
    columns_ref, bias_ref, out_ref, acts_ref, back_ref, sems = refs[8:]
    lat, core = lax.axis_index("lat"), lax.axis_index("ckpt")
    tiles, _, depth = columns_ref.shape
    for place in range(4):
        for ref, holder in ((mine[place], core), (theirs[place], 1 - core)):
            slots = ((0, holder), (4 + 8 * holder, 0), (4 + 8 * holder, 1), (8, holder))
            for slot, (mask, which) in enumerate(slots):
                source = lat ^ place ^ mask
                owner = source ^ (4 * which)
                for index in range(2):
                    tile = (source // 4) ^ (2 * index)
                    row = pl.multiple_of(tile * depth + owner * BLOCK, BLOCK)
                    acts_ref[pl.ds(row, BLOCK), :] = ref[slot, index]

    def give(tile):
        lanes = pl.ds(tile * TILE, TILE)
        return pltpu.make_async_copy(back_ref.at[tile], out_ref.at[:, lanes], sems.at[tile])

    for tile in range(tiles):
        acts = acts_ref[tile * depth : (tile + 1) * depth, :]
        total = jnp.dot(columns_ref[tile], acts, preferred_element_type=F32)
        back_ref[tile] = (total + bias_ref[...]).astype(BF16)
        give(tile).start()
    for tile in range(tiles):
        give(tile).wait()


def decode(mine, theirs, columns, dec_bias):
    tiles, features, depth = columns.shape
    return pl.pallas_call(
        decode_kernel,
        out_shape=jax.ShapeDtypeStruct((features, tiles * TILE), BF16),
        in_specs=[VMEM] * 10,
        out_specs=ANY,
        scratch_shapes=[
            pltpu.VMEM((tiles * depth, TILE), BF16),
            pltpu.VMEM((tiles, features, TILE), BF16),
            pltpu.SemaphoreType.DMA((tiles,)),
        ],
        compiler_params=params(VMEM_SMALL),
        cost_estimate=cost(2 * tiles * features * depth * TILE, 4 * 2**20),
        name="decode",
    )(*mine, *theirs, columns, dec_bias)


def body_planes(inputs, enc_weight, enc_bias, dec_weight, dec_bias, block_ids, live):
    owners = lax.axis_size("lat")
    core = lax.axis_index("ckpt")

    def swap(values, mask):
        return lax.ppermute(values, "lat", [(i, i ^ mask) for i in range(owners)])

    def across(values):
        return lax.ppermute(values, "ckpt", [(0, 1), (1, 0)])

    near_own = inputs[0]
    near = [near_own] + [swap(near_own, place) for place in range(1, 4)]
    bias = enc_bias.reshape(-1, PAIR)
    depth = enc_weight.shape[1]
    first = send_columns(block_ids, enc_weight[0], [], 0, FIRST, near_own.shape, 512)
    plane = lax.axis_index("lat") // 4
    at_end = (plane == 0) | (plane == 3)

    def rotate(values, end_mask, middle_mask):
        pairs = [(i, i ^ (end_mask if i // 4 in (0, 3) else middle_mask)) for i in range(owners)]
        return lax.ppermute(values, "lat", pairs)

    one = rotate(jnp.where(at_end, first, near_own), 4, 8)
    two = rotate(jnp.where(at_end, near_own, first), 8, 4)
    rest = send_columns(block_ids, enc_weight[0], [bias], FIRST, depth - FIRST, (depth - FIRST + EXTRA, PAIR), 512)
    rest, one = lax.optimization_barrier((rest, one))
    rest = swap(rest, 4)
    far_own = jnp.where(at_end, one, two)
    first = jnp.where(at_end, two, one)
    own = own_columns(block_ids, enc_weight[0])
    columns = stage_decoder(block_ids, dec_weight[0])
    far = [far_own] + [swap(far_own, place) for place in range(1, 4)]

    partial = encode(block_ids, live, near, far, own, first, rest, bias)
    partial, columns = lax.optimization_barrier((partial, columns))
    acts = jnp.maximum(partial + across(partial), 0.0).astype(BF16).reshape(2, 2, BLOCK, TILE)

    ends = [(2 * i, 2 * (i ^ 4)) for i in range(owners)] + [(2 * i + 1, 2 * (i ^ 12) + 1) for i in range(owners)]
    along = lax.ppermute(acts, ("lat", "ckpt"), ends)
    mine_half = lax.dynamic_slice_in_dim(acts, core, 1, 0)
    middle = swap(mine_half, 8)
    payload = jnp.concatenate([mine_half, along, middle], axis=0)
    mine = [payload] + [swap(payload, place) for place in range(1, 4)]
    theirs = [across(values) for values in mine]
    recon = decode(mine, theirs, columns, dec_bias.reshape(-1, 1))
    return recon[None]


def body(inputs, enc_weight, enc_bias, dec_weight, dec_bias, block_ids, live):
    tiles, owners = block_ids.shape
    cores = lax.axis_size("ckpt")
    if owners == 16 and cores == 2 and tiles == 4 and inputs.shape[:2] == (1, tiles * TILE // owners):
        return body_planes(inputs, enc_weight, enc_bias, dec_weight, dec_bias, block_ids, live)
    return body_any(inputs, enc_weight, enc_bias, dec_weight, dec_bias, block_ids, live)


def solution(mesh):
    placed = (
        P("ckpt", ("groups", "lat"), None),
        P("ckpt", None, "lat"),
        P("lat"),
        P("ckpt", "lat", None),
        P("ckpt", "lat"),
        P("groups", None),
        P("groups", None),
    )
    return jax.shard_map(
        body, mesh=mesh, in_specs=placed, out_specs=P("ckpt", "lat", "groups"), check_vma=False
    )
```

```python
import functools

import jax
import jax.numpy as jnp
from jax import lax
from jax.experimental import pallas as pl
from jax.experimental.pallas import tpu as pltpu
from jax.sharding import PartitionSpec as P

BLOCK = 64
TILE = 128
PAIR = 2 * BLOCK
EXTRA = 16
FIRST = 1024
F32 = jnp.float32
BF16 = jnp.bfloat16
VMEM_WEIGHTS = 50 * 1024 * 1024
VMEM_SMALL = 12 * 1024 * 1024


def body_any(inputs, enc_weight, enc_bias, dec_weight, dec_bias, block_ids, live):
    lat_count = lax.axis_size("lat")
    lat_index = lax.axis_index("lat")
    lat_dev = enc_weight.shape[2]
    own_blocks = lat_dev // BLOCK
    local_ckpts = dec_weight.shape[0]
    features = dec_weight.shape[1]
    preact = jnp.einsum(
        "cdl,crd->lr",
        enc_weight,
        lax.all_gather(inputs, "lat", axis=1, tiled=True),
        preferred_element_type=F32,
    )
    token_count = preact.shape[1]
    tiles = token_count // TILE
    own_ids = lax.dynamic_slice_in_dim(block_ids, lat_index, 1, 1)[:, 0]
    own_live = lax.dynamic_slice_in_dim(live, lat_index, 1, 1)[:, 0]
    choose = (own_ids[:, None] == jnp.arange(own_blocks, dtype=jnp.int32)[None, :]) & (own_live[:, None] == 1)
    choose_cols = jnp.transpose(choose.astype(F32))
    grouped_vals = preact.reshape(own_blocks, BLOCK, tiles, TILE)
    picked = jnp.sum(grouped_vals * choose_cols[:, None, :, None], axis=0)
    picked_bias = jnp.einsum("pe,pt->et", enc_bias.reshape(own_blocks, BLOCK), choose_cols, precision=lax.Precision.HIGHEST)
    summed = lax.psum(picked, "ckpt") + picked_bias[:, :, None]
    acts = jnp.transpose(jnp.maximum(summed, 0.0), (1, 0, 2)).astype(BF16)
    onehot = (
        (block_ids[:, :, None] == jnp.arange(own_blocks, dtype=jnp.int32)[None, None, :]) & (live[:, :, None] == 1)
    ).astype(BF16)
    grouped = dec_weight.reshape(local_ckpts, features, lat_count, own_blocks, BLOCK)
    selected = jnp.einsum("tnp,cdnpe->cdtne", onehot, grouped, preferred_element_type=F32).astype(BF16)
    total = jnp.einsum(
        "ntes,cdtne->cdts",
        lax.all_gather(acts[None], "lat", axis=0, tiled=True),
        selected,
        preferred_element_type=F32,
    )
    recon = total.reshape(local_ckpts, features, token_count)
    return (recon + dec_bias[:, :, None]).astype(BF16)


def swap_if(flag, values):
    return jnp.where(flag, pltpu.roll(values, BLOCK, 1), values)


def side_by_side(first, first_odd, second, second_odd):
    lane = lax.broadcasted_iota(jnp.int32, first.shape, 1)
    return jnp.where(lane < BLOCK, swap_if(first_odd == 1, first), swap_if(second_odd == 0, second))


def column_of(block):
    return pl.ds(pl.multiple_of((block // 2) * PAIR, PAIR), PAIR)


SMEM = pl.BlockSpec(memory_space=pltpu.SMEM)
VMEM = pl.BlockSpec(memory_space=pltpu.VMEM)
ANY = pl.BlockSpec(memory_space=pl.ANY)


def params(limit=VMEM_WEIGHTS):
    return pltpu.CompilerParams(vmem_limit_bytes=limit)


def cost(flops, moved):
    return pl.CostEstimate(flops=flops, bytes_accessed=moved, transcendentals=0)


def send_columns_kernel(all_ids_ref, weight_ref, *refs, step, base):
    *bias_refs, out_ref, in_ref, ids_ref, ids_sem, sems = refs
    ids_copy = pltpu.make_async_copy(all_ids_ref, ids_ref, ids_sem)
    ids_copy.start()
    ids_copy.wait()
    lat = lax.axis_index("lat")
    plane = lat // 4
    depth = in_ref.shape[1]
    chunks = depth // step
    folded = out_ref.shape[1] > PAIR
    blocks = [ids_ref[plane ^ mask, lat] for mask in (1, 3)]
    odds = [block % 2 for block in blocks]

    def fetch(chunk, which):
        source = weight_ref.at[pl.ds(base + chunk * step, step), column_of(blocks[which])]
        return pltpu.make_async_copy(source, in_ref.at[which, pl.ds(chunk * step, step)], sems.at[which, chunk])

    for chunk in range(chunks):
        for which in range(2):
            fetch(chunk, which).start()

    if bias_refs:
        (bias_ref,) = bias_refs
        extra = out_ref.shape[0] - depth
        parts = [bias_ref[pl.ds(block // 2, 1), :] for block in blocks]
        bias = side_by_side(parts[0], odds[0], parts[1], odds[1])
        high = bias.astype(BF16)
        middle = (bias - high.astype(F32)).astype(BF16)
        low = (bias - high.astype(F32) - middle.astype(F32)).astype(BF16)
        row = lax.broadcasted_iota(jnp.int32, (extra, PAIR), 0)
        rows = jnp.zeros((extra, PAIR), F32)
        for index, part in enumerate((high, middle, low)):
            rows = jnp.where(row == index, jnp.broadcast_to(part.astype(F32), rows.shape), rows)
        out_ref[depth:, :] = rows.astype(BF16)

    for chunk in range(chunks):
        for which in range(2):
            fetch(chunk, which).wait()
        rows = slice(chunk * step, (chunk + 1) * step)
        both = side_by_side(in_ref[0, rows, :].astype(F32), odds[0], in_ref[1, rows, :].astype(F32), odds[1])
        both = both.astype(BF16)
        if folded:
            high = out_ref.shape[0]
            for piece in range(step // high):
                left = (chunk * (step // high) + piece) * PAIR
                out_ref[:, left : left + PAIR] = both[piece * high : (piece + 1) * high, :]
        else:
            out_ref[rows, :] = both


def send_columns(ids, enc_weight, bias, base, depth, shape, step):
    return pl.pallas_call(
        functools.partial(send_columns_kernel, step=step, base=base),
        out_shape=jax.ShapeDtypeStruct(shape, BF16),
        in_specs=[ANY, ANY] + [VMEM] * len(bias),
        out_specs=VMEM,
        scratch_shapes=[
            pltpu.VMEM((2, depth, PAIR), BF16),
            pltpu.SMEM(ids.shape, jnp.int32),
            pltpu.SemaphoreType.DMA,
            pltpu.SemaphoreType.DMA((2, depth // step)),
        ],
        compiler_params=params(),
        cost_estimate=cost(0, 3 * depth * PAIR * 2),
        name="send_columns",
    )(ids, enc_weight, *bias)


def own_columns_kernel(ids_ref, weight_ref, out_ref, sems, *, step):
    lat = lax.axis_index("lat")
    copies = []
    for index in range(2):
        lanes = column_of(ids_ref[(lat // 4) ^ (2 * index), lat])
        for chunk in range(out_ref.shape[1] // step):
            rows = pl.ds(chunk * step, step)
            copies.append(
                pltpu.make_async_copy(weight_ref.at[rows, lanes], out_ref.at[index, rows], sems.at[index, chunk])
            )
    for copy in copies:
        copy.start()
    for copy in copies:
        copy.wait()


def own_columns(ids, enc_weight):
    depth = enc_weight.shape[0]
    step = 1024
    return pl.pallas_call(
        functools.partial(own_columns_kernel, step=step),
        out_shape=jax.ShapeDtypeStruct((2, depth, PAIR), BF16),
        in_specs=[SMEM, ANY],
        out_specs=VMEM,
        scratch_shapes=[pltpu.SemaphoreType.DMA((2, depth // step))],
        compiler_params=params(),
        cost_estimate=cost(0, 4 * depth * PAIR * 2),
        name="own_columns",
    )(ids, enc_weight)


def encode_kernel(ids_ref, live_ref, *refs):
    near = refs[0:4]
    far = refs[4:8]
    own_ref, first_ref, rest_ref, bias_ref, out_ref, turn_ref, flip_ref = refs[8:]
    lat, core = lax.axis_index("lat"), lax.axis_index("ckpt")
    plane, place = lat // 4, lat % 4
    depth = own_ref.shape[1]
    shard = TILE // 4
    step = 1024
    parts = rest_ref[depth - FIRST :, :].astype(F32)
    other_bias = (parts[0:1] + parts[1:2]) + parts[2:3]
    for index, tokens in enumerate((near, far)):
        total = jnp.zeros((TILE, 2 * PAIR), F32)
        for start in range(0, depth, step):
            rows = jnp.concatenate([ref[:, start : start + step] for ref in tokens], axis=0)
            if start < FIRST:
                pieces = range(start // shard, (start + step) // shard)
                partner = jnp.concatenate([first_ref[:, i * PAIR : (i + 1) * PAIR] for i in pieces], axis=0)
            else:
                partner = rest_ref[start - FIRST : start - FIRST + step, :]
            columns = jnp.concatenate([own_ref[index, start : start + step, :], partner], axis=1)
            total += jnp.dot(rows, columns, preferred_element_type=F32)
        tile = plane ^ (2 * index)
        block = ids_ref[tile, lat]
        bias = jnp.concatenate([bias_ref[pl.ds(block // 2, 1), :], other_bias], axis=1)
        total += jnp.where(core == 0, bias, 0.0)
        for turn in range(4):
            to = pl.ds(pl.multiple_of((place ^ turn) * shard, shard), shard)
            turn_ref[to, :] = total[turn * shard : (turn + 1) * shard, :]
        flip_ref[...] = jnp.transpose(turn_ref[:, :PAIR])
        own = flip_ref[pl.ds(pl.multiple_of((block % 2) * BLOCK, BLOCK), BLOCK), :]
        other = jnp.transpose(turn_ref[:, PAIR:])[index * BLOCK : (index + 1) * BLOCK, :]
        out_ref[index] = jnp.where(live_ref[tile, lat] == 1, own, 0.0)
        out_ref[2 + index] = jnp.where(live_ref[tile, lat ^ 4] == 1, other, 0.0)


def encode(ids, live, near, far, own, first, rest, bias):
    return pl.pallas_call(
        encode_kernel,
        out_shape=jax.ShapeDtypeStruct((4, BLOCK, TILE), F32),
        in_specs=[SMEM, SMEM] + [VMEM] * 12,
        out_specs=VMEM,
        scratch_shapes=[pltpu.VMEM((TILE, 2 * PAIR), F32), pltpu.VMEM((PAIR, TILE), F32)],
        compiler_params=params(VMEM_SMALL),
        cost_estimate=cost(4 * TILE * own.shape[1] * 2 * PAIR, 5 * 2**20),
        name="encode",
    )(ids, live, *near, *far, own, first, rest, bias)


def stage_decoder_kernel(ids_ref, weight_ref, out_ref, in_ref, sems):
    tiles, owners = ids_ref.shape
    span = weight_ref.shape[1] // owners

    def fetch(tile, owner):
        lanes = pl.ds(pl.multiple_of(owner * span + (ids_ref[tile, owner] // 2) * PAIR, PAIR), PAIR)
        return pltpu.make_async_copy(weight_ref.at[:, lanes], in_ref.at[tile, owner], sems.at[tile, owner])

    for tile in range(tiles):
        for owner in range(owners):
            fetch(tile, owner).start()
    for tile in range(tiles):
        for owner in range(0, owners, 2):
            fetch(tile, owner).wait()
            fetch(tile, owner + 1).wait()
            both = side_by_side(
                in_ref[tile, owner].astype(F32),
                ids_ref[tile, owner] % 2,
                in_ref[tile, owner + 1].astype(F32),
                ids_ref[tile, owner + 1] % 2,
            )
            out_ref[tile, :, owner * BLOCK : owner * BLOCK + PAIR] = both.astype(BF16)


def stage_decoder(ids, dec_weight):
    tiles, owners = ids.shape
    features = dec_weight.shape[0]
    return pl.pallas_call(
        stage_decoder_kernel,
        out_shape=jax.ShapeDtypeStruct((tiles, features, owners * BLOCK), BF16),
        in_specs=[SMEM, ANY],
        out_specs=VMEM,
        scratch_shapes=[
            pltpu.VMEM((tiles, owners, features, PAIR), BF16),
            pltpu.SemaphoreType.DMA((tiles, owners)),
        ],
        compiler_params=params(),
        cost_estimate=cost(0, 6 * tiles * features * owners * BLOCK),
        name="stage_decoder",
    )(ids, dec_weight)


def decode_kernel(*refs):
    mine = refs[0:4]
    theirs = refs[4:8]
    columns_ref, bias_ref, out_ref, acts_ref, back_ref, sems = refs[8:]
    lat, core = lax.axis_index("lat"), lax.axis_index("ckpt")
    tiles, _, depth = columns_ref.shape
    for place in range(4):
        for ref, holder in ((mine[place], core), (theirs[place], 1 - core)):
            slots = ((0, holder), (4 + 8 * holder, 0), (4 + 8 * holder, 1), (8, holder))
            for slot, (mask, which) in enumerate(slots):
                source = lat ^ place ^ mask
                owner = source ^ (4 * which)
                for index in range(2):
                    tile = (source // 4) ^ (2 * index)
                    row = pl.multiple_of(tile * depth + owner * BLOCK, BLOCK)
                    acts_ref[pl.ds(row, BLOCK), :] = ref[slot, index]

    def give(tile):
        lanes = pl.ds(tile * TILE, TILE)
        return pltpu.make_async_copy(back_ref.at[tile], out_ref.at[:, lanes], sems.at[tile])

    for tile in range(tiles):
        acts = acts_ref[tile * depth : (tile + 1) * depth, :]
        total = jnp.dot(columns_ref[tile], acts, preferred_element_type=F32)
        back_ref[tile] = (total + bias_ref[...]).astype(BF16)
        give(tile).start()
    for tile in range(tiles):
        give(tile).wait()


def decode(mine, theirs, columns, dec_bias):
    tiles, features, depth = columns.shape
    return pl.pallas_call(
        decode_kernel,
        out_shape=jax.ShapeDtypeStruct((features, tiles * TILE), BF16),
        in_specs=[VMEM] * 10,
        out_specs=ANY,
        scratch_shapes=[
            pltpu.VMEM((tiles * depth, TILE), BF16),
            pltpu.VMEM((tiles, features, TILE), BF16),
            pltpu.SemaphoreType.DMA((tiles,)),
        ],
        compiler_params=params(VMEM_SMALL),
        cost_estimate=cost(2 * tiles * features * depth * TILE, 4 * 2**20),
        name="decode",
    )(*mine, *theirs, columns, dec_bias)


def body_planes(inputs, enc_weight, enc_bias, dec_weight, dec_bias, block_ids, live):
    owners = lax.axis_size("lat")
    core = lax.axis_index("ckpt")

    def swap(values, mask):
        return lax.ppermute(values, "lat", [(i, i ^ mask) for i in range(owners)])

    def across(values):
        return lax.ppermute(values, "ckpt", [(0, 1), (1, 0)])

    near_own = inputs[0]
    near = [near_own] + [swap(near_own, place) for place in range(1, 4)]
    bias = enc_bias.reshape(-1, PAIR)
    depth = enc_weight.shape[1]
    first = send_columns(block_ids, enc_weight[0], [], 0, FIRST, near_own.shape, 512)
    plane = lax.axis_index("lat") // 4
    at_end = (plane == 0) | (plane == 3)

    def rotate(values, end_mask, middle_mask):
        pairs = [(i, i ^ (end_mask if i // 4 in (0, 3) else middle_mask)) for i in range(owners)]
        return lax.ppermute(values, "lat", pairs)

    one = rotate(jnp.where(at_end, first, near_own), 4, 8)
    two = rotate(jnp.where(at_end, near_own, first), 8, 4)
    rest = send_columns(block_ids, enc_weight[0], [bias], FIRST, depth - FIRST, (depth - FIRST + EXTRA, PAIR), 512)
    rest, one = lax.optimization_barrier((rest, one))
    rest = swap(rest, 4)
    far_own = jnp.where(at_end, one, two)
    first = jnp.where(at_end, two, one)
    own = own_columns(block_ids, enc_weight[0])
    columns = stage_decoder(block_ids, dec_weight[0])
    far = [far_own] + [swap(far_own, place) for place in range(1, 4)]

    partial = encode(block_ids, live, near, far, own, first, rest, bias)
    partial, columns = lax.optimization_barrier((partial, columns))
    acts = jnp.maximum(partial + across(partial), 0.0).astype(BF16).reshape(2, 2, BLOCK, TILE)

    ends = [(2 * i, 2 * (i ^ 4)) for i in range(owners)] + [(2 * i + 1, 2 * (i ^ 12) + 1) for i in range(owners)]
    along = lax.ppermute(acts, ("lat", "ckpt"), ends)
    mine_half = lax.dynamic_slice_in_dim(acts, core, 1, 0)
    middle = swap(mine_half, 8)
    payload = jnp.concatenate([mine_half, along, middle], axis=0)
    other = across(payload)
    diagonal = swap(payload, 3)
    payload, other = lax.optimization_barrier((payload, other))
    mine = [payload, swap(payload, 1), swap(payload, 2), diagonal]
    theirs = [other] + [across(values) for values in mine[1:]]
    recon = decode(mine, theirs, columns, dec_bias.reshape(-1, 1))
    return recon[None]


def body(inputs, enc_weight, enc_bias, dec_weight, dec_bias, block_ids, live):
    tiles, owners = block_ids.shape
    cores = lax.axis_size("ckpt")
    if owners == 16 and cores == 2 and tiles == 4 and inputs.shape[:2] == (1, tiles * TILE // owners):
        return body_planes(inputs, enc_weight, enc_bias, dec_weight, dec_bias, block_ids, live)
    return body_any(inputs, enc_weight, enc_bias, dec_weight, dec_bias, block_ids, live)


def solution(mesh):
    placed = (
        P("ckpt", ("groups", "lat"), None),
        P("ckpt", None, "lat"),
        P("lat"),
        P("ckpt", "lat", None),
        P("ckpt", "lat"),
        P("groups", None),
        P("groups", None),
    )
    return jax.shard_map(
        body, mesh=mesh, in_specs=placed, out_specs=P("ckpt", "lat", "groups"), check_vma=False
    )
```
